32 devices in a mesh: groups: 1, kcol: 16 (over z, y, x), qrow: 2 (over core).
Axes of the slice: x: 2, y: 2, z: 4, core: 2. Of those that a mesh axis runs over, the one named last changes fastest.
Arguments:
- queries: bfloat16 [128, 1024], P(('groups', 'kcol', 'qrow')), may hold values from -120 to 120
- key_value: bfloat16 [24576, 256], P(('groups', 'kcol')), may hold values from -6 to 6
- block_lists: int32 [1, 64], P('groups'), may hold values from 0 to 191, as said below
Outputs:
- attended: bfloat16 [128, 1024], P(('groups', 'kcol', 'qrow'))
The draws below stay inside these ranges and needn't reach their ends.
Inputs may be any that keep to these rules, and one draw needn't show every extreme that they name: `block_lists`: row i names 64 distinct key blocks, none after block 191 + i (the block that holds query block i); it always names that block, the 11 blocks just before it, and block 0.
All inputs are finite; a program needn't handle non-finite values.
Results may differ from the reference program's by a relative error of at most 0.0065.
Values may be sent and summed in bfloat16 or wider, within the bound.
A program may use at most 128 MiB of HBM per device.

```python
import math
import jax
import jax.numpy as jnp
from jax import lax

HD = 128
HEADS = 8
BLK = 128
KB_DEV = 12
KB = 192
QTOK = 128
QB = 1
NSEL = 64


def draw_pairs(key):
    key_rows = jnp.clip(jax.random.normal(jax.random.fold_in(key, 11), (KB * BLK, HD), jnp.float32), -6.0, 6.0)
    value_rows = jnp.clip(jax.random.normal(jax.random.fold_in(key, 12), (KB * BLK, HD), jnp.float32), -6.0, 6.0)
    return (key_rows, value_rows)


def draw_key_value(key, part):
    key_rows, value_rows = draw_pairs(key)
    return jnp.concatenate([key_rows, value_rows], axis=1).astype(jnp.bfloat16)


def draw_queries(key, part):
    drawn = 3.0 * jnp.clip(jax.random.normal(jax.random.fold_in(key, 14), (QTOK, HEADS, HD), jnp.float32), -6.0, 6.0)
    return drawn.reshape(QTOK, HEADS * HD).astype(jnp.bfloat16)


def draw_block_lists(key, part):
    popular = (jax.random.randint(jax.random.fold_in(key, 21), (KB,), 0, 4) == 0).astype(jnp.int32)
    row_noise = jax.random.randint(jax.random.fold_in(key, 22), (QB, KB), 0, 65536)
    candidates = jnp.arange(KB, dtype=jnp.int32)

    def one_row(block_index, noise_row):
        limit = KB - QB + block_index - KB_DEV + 1
        score = (popular * 65536 + noise_row) * 4096 + candidates
        score = jnp.where(candidates == 0, 2 ** 30, score)
        score = jnp.where(candidates < limit, score, -1 - candidates)
        unused, picked = lax.top_k(score, NSEL - KB_DEV)
        window = limit + jnp.arange(KB_DEV, dtype=jnp.int32)
        return jnp.concatenate([picked.astype(jnp.int32), window])
    return jax.vmap(one_row)(jnp.arange(QB, dtype=jnp.int32), row_noise)


def setup_inputs(seed: int = 0, part: int = 0) -> dict:
    splits = jax.random.split(jax.random.key(seed), 4)
    own_keys = jax.random.split(jax.random.fold_in(splits[3], part), 4)
    return {
        "queries": draw_queries(jax.random.fold_in(jax.random.fold_in(splits[3], part), 71), part),
        "key_value": draw_key_value(jax.random.fold_in(jax.random.fold_in(splits[3], part), 71), part),
        "block_lists": draw_block_lists(jax.random.fold_in(jax.random.fold_in(splits[3], part), 71), part),
    }


masked_score = -1e+30

def reference(queries, key_value, block_lists):
    score_scale = 1.0 / math.sqrt(HD)
    blocks = key_value.reshape(KB, BLK, 2 * HD)
    offset = (KB - QB) * BLK
    query_tiles = queries.reshape(QB, BLK, HEADS, HD)

    def one_block(inputs):
        query_tile, listed, block_index = inputs
        chosen = jnp.take(blocks, listed, axis=0).reshape(NSEL * BLK, 2 * HD).astype(jnp.float32)
        key_pos = (listed[:, None] * BLK + jnp.arange(BLK, dtype=jnp.int32)[None, :]).reshape(-1)
        query_pos = offset + block_index * BLK + jnp.arange(BLK, dtype=jnp.int32)
        visible = key_pos[None, :] <= query_pos[:, None]
        scores = jnp.einsum('thd,kd->htk', query_tile.astype(jnp.float32), chosen[:, :HD], precision=lax.Precision.HIGHEST) * score_scale
        scores = jnp.where(visible[None], scores, masked_score)
        row_max = lax.optimization_barrier(jnp.max(scores, axis=-1))
        weights = jnp.where(visible[None], jnp.exp(scores - row_max[..., None]), 0.0)
        row_total = lax.optimization_barrier(jnp.sum(weights, axis=-1))
        rounded = lax.optimization_barrier(weights.astype(jnp.bfloat16)).astype(jnp.float32)
        numerator = jnp.einsum('htk,kd->thd', rounded, chosen[:, HD:], precision=lax.Precision.HIGHEST)
        result = numerator / jnp.transpose(row_total)[..., None]
        return result.reshape(BLK, HEADS * HD).astype(jnp.bfloat16)
    attended = lax.map(one_block, (query_tiles, block_lists, jnp.arange(QB, dtype=jnp.int32)))
    return attended.reshape(QTOK, HEADS * HD)
```

```python
import functools
import math

import jax
import jax.numpy as jnp
from jax import lax
from jax.experimental import pallas as pl
from jax.experimental.pallas import tpu as pltpu
from jax.sharding import PartitionSpec as P

BLK = 128
LANES = 128
MASKED = -(2.0**100)
VMEM_LIMIT = 127 * 512 * 1024


def kernel(
    columns,
    cores,
    q_ref,
    kv_hbm,
    lists_ref,
    out_ref,
    kv,
    q_all,
    bias,
    numer,
    stats,
    numer_in,
    stats_in,
    kv_sem,
    q_send,
    q_recv,
    n_send,
    n_recv,
    s_send,
    s_recv,
):
    me = lax.axis_index("kcol")
    core = lax.axis_index("qrow")
    tok_dev, features = q_ref.shape
    head_dim = kv.shape[1] // 2
    heads = features // head_dim
    stored = kv.shape[0] // BLK
    all_blocks = stored * columns
    query_blocks = lists_ref.shape[0]
    rows = tok_dev * heads
    unit_cols = LANES // rows
    units = columns // unit_cols
    tile_cols = BLK // cores // tok_dev
    scale = math.log2(math.e) / math.sqrt(head_dim)

    kv_copy = pltpu.make_async_copy(kv_hbm, kv, kv_sem)
    kv_copy.start()

    barrier = pltpu.get_barrier_semaphore()
    for step in range(1, columns):
        pl.semaphore_signal(
            barrier, inc=1, device_id={"kcol": lax.rem(me + step, columns)}
        )

    def rows_of(column):
        return pl.ds(pl.multiple_of(column * rows, rows), rows)

    own = q_ref[...].astype(jnp.float32)
    own = jnp.concatenate(
        [own[:, h * head_dim : (h + 1) * head_dim] for h in range(heads)], axis=0
    )
    q_all[rows_of(me), :] = own.astype(jnp.bfloat16)

    for tile in range(query_blocks):
        listed = lists_ref[tile : tile + 1, :]
        for block in range(stored):
            hit = jnp.where(listed == me * stored + block, 0.0, MASKED)
            hit = jnp.max(hit, axis=1, keepdims=True)
            bias[tile, :, block * BLK : (block + 1) * BLK] = jnp.broadcast_to(hit, (8, BLK))

    pl.semaphore_wait(barrier, columns - 1)

    my_unit = me // unit_cols
    my_place = lax.rem(me, unit_cols)

    def unit_at(g):
        return lax.rem(my_unit + g, units)

    def column_at(g, j):
        return unit_at(g) * unit_cols + lax.rem(my_place + j, unit_cols)

    def q_copy(peer):
        return pltpu.make_async_remote_copy(
            src_ref=q_all.at[rows_of(me)],
            dst_ref=q_all.at[rows_of(me)],
            send_sem=q_send.at[peer],
            recv_sem=q_recv.at[me],
            device_id={"kcol": peer},
        )

    def q_landed(source):
        return pltpu.make_async_remote_copy(
            src_ref=q_all.at[rows_of(source)],
            dst_ref=q_all.at[rows_of(source)],
            send_sem=q_send.at[source],
            recv_sem=q_recv.at[source],
            device_id={"kcol": source},
        )

    def n_copy(peer, source):
        return pltpu.make_async_remote_copy(
            src_ref=numer.at[rows_of(peer)],
            dst_ref=numer_in.at[rows_of(source)],
            send_sem=n_send.at[peer],
            recv_sem=n_recv.at[source],
            device_id={"kcol": peer},
        )

    def s_copy(peer, source):
        return pltpu.make_async_remote_copy(
            src_ref=stats.at[peer // unit_cols],
            dst_ref=stats_in.at[source],
            send_sem=s_send.at[peer],
            recv_sem=s_recv.at[source],
            device_id={"kcol": peer},
        )

    peers = [(g, j) for g in range(units) for j in range(unit_cols) if g or j]
    for g, j in peers:
        q_copy(column_at(units - g if g else 0, j)).start()

    row_id = lax.broadcasted_iota(jnp.int32, (LANES, LANES), 0)
    lane_id = lax.broadcasted_iota(jnp.int32, (LANES, LANES), 1)
    diagonal = row_id == lane_id
    row_token = core * tok_dev + lax.rem(row_id, tok_dev)
    row_column = row_id // rows

    kv_copy.wait()

    for g in range(units):
        unit = unit_at(g)
        for j in range(unit_cols):
            if g or j:
                q_landed(column_at(g, j)).wait_recv()
        tile = unit * unit_cols // tile_cols
        unit_rows = pl.ds(pl.multiple_of(unit * LANES, LANES), LANES)
        scores = lax.dot_general(
            q_all[unit_rows, :],
            kv[:, :head_dim],
            (((1,), (1,)), ((), ())),
            preferred_element_type=jnp.float32,
        )
        query_pos = (
            (all_blocks - query_blocks) * BLK
            + (unit * unit_cols + row_column) * (cores * tok_dev)
            + row_token
        )
        parts = []
        for block in range(stored):
            part = scores[:, block * BLK : (block + 1) * BLK]
            part = part + bias[tile, 0:1, block * BLK : (block + 1) * BLK]
            if block >= stored - query_blocks:
                key_pos = (me * stored + block) * BLK + lane_id
                part = jnp.where(key_pos <= query_pos, part, MASKED)
            parts.append(part)
        row_max = functools.reduce(jnp.maximum, parts)
        row_max = jnp.max(row_max, axis=1, keepdims=True)
        weights = [jnp.exp2((part - row_max) * scale) for part in parts]
        row_total = jnp.sum(functools.reduce(jnp.add, weights), axis=1, keepdims=True)
        summed = lax.dot_general(
            jnp.concatenate([w.astype(jnp.bfloat16) for w in weights], axis=1),
            kv[:, head_dim:],
            (((1,), (0,)), ((), ())),
            preferred_element_type=jnp.float32,
        )
        numer[unit_rows, :] = summed.astype(jnp.bfloat16)
        stats[unit, 0:1, :] = jnp.sum(jnp.where(diagonal, row_max, 0.0), axis=0, keepdims=True)
        stats[unit, 1:2, :] = jnp.sum(jnp.where(diagonal, row_total, 0.0), axis=0, keepdims=True)
        for j in range(unit_cols):
            if g or j:
                n_copy(column_at(g, j), me).start()
                s_copy(column_at(g, j), me).start()

    numer_in[rows_of(me), :] = numer[rows_of(me), :]
    stats_in[me] = stats[my_unit]

    for g, j in peers:
        source = column_at(units - g if g else 0, j)
        s_copy(source, source).wait_recv()
    every_max = stats_in[:, 0, :]
    every_total = stats_in[:, 1, :]
    top = jnp.max(every_max, axis=0, keepdims=True)
    factor = jnp.exp2((every_max - top) * scale)
    factor = factor / jnp.sum(factor * every_total, axis=0, keepdims=True)
    pad = -columns % LANES
    if pad:
        factor = jnp.concatenate([factor, jnp.zeros((pad, LANES), jnp.float32)], axis=0)
    factor = jnp.transpose(factor)
    turned = jnp.zeros((rows, LANES), jnp.float32)
    for place in range(unit_cols):
        turned = jnp.where(my_place == place, factor[place * rows : (place + 1) * rows, :], turned)

    for g, j in peers:
        source = column_at(units - g if g else 0, j)
        n_copy(source, source).wait_recv()
    total = jnp.zeros((rows, head_dim), jnp.float32)
    for source in range(columns):
        arrived = numer_in[source * rows : (source + 1) * rows, :].astype(jnp.float32)
        total = total + arrived * turned[:, source : source + 1]
    out_ref[...] = jnp.concatenate(
        [total[h * tok_dev : (h + 1) * tok_dev, :] for h in range(heads)], axis=1
    ).astype(out_ref.dtype)

    for g, j in peers:
        peer = column_at(g, j)
        q_copy(peer).wait_send()
        n_copy(peer, me).wait_send()
        s_copy(peer, me).wait_send()


def per_device(columns, cores, queries, key_value, block_lists):
    tok_dev, features = queries.shape
    head_dim = key_value.shape[1] // 2
    all_rows = columns * tok_dev * (features // head_dim)
    query_blocks = block_lists.shape[0]
    units = all_rows // LANES
    dma = pltpu.SemaphoreType.DMA
    vmem = pl.BlockSpec(memory_space=pltpu.VMEM)
    return pl.pallas_call(
        functools.partial(kernel, columns, cores),
        out_shape=jax.ShapeDtypeStruct((tok_dev, features), jnp.bfloat16),
        in_specs=[vmem, pl.BlockSpec(memory_space=pl.ANY), vmem],
        out_specs=vmem,
        scratch_shapes=[
            pltpu.VMEM(key_value.shape, jnp.bfloat16),
            pltpu.VMEM((all_rows, head_dim), jnp.bfloat16),
            pltpu.VMEM((query_blocks, 8, key_value.shape[0]), jnp.float32),
            pltpu.VMEM((all_rows, head_dim), jnp.bfloat16),
            pltpu.VMEM((units, 2, LANES), jnp.float32),
            pltpu.VMEM((all_rows, head_dim), jnp.bfloat16),
            pltpu.VMEM((columns, 2, LANES), jnp.float32),
            dma,
            dma((columns,)),
            dma((columns,)),
            dma((columns,)),
            dma((columns,)),
            dma((columns,)),
            dma((columns,)),
        ],
        compiler_params=pltpu.CompilerParams(
            collective_id=0, has_side_effects=True, vmem_limit_bytes=VMEM_LIMIT
        ),
    )(queries, key_value, block_lists)


def solution(mesh):
    placed = (P(("groups", "kcol", "qrow"), None), P(("groups", "kcol"), None), P("groups", None))
    return jax.shard_map(
        functools.partial(per_device, mesh.shape["kcol"], mesh.shape["qrow"]),
        mesh=mesh,
        in_specs=placed,
        out_specs=P(("groups", "kcol", "qrow"), None),
        check_vma=False,
    )
```

```python
import functools
import math

import jax
import jax.numpy as jnp
from jax import lax
from jax.experimental import pallas as pl
from jax.experimental.pallas import tpu as pltpu
from jax.sharding import PartitionSpec as P

BLK = 128
LANES = 128
MASKED = -(2.0**100)
VMEM_LIMIT = 127 * 512 * 1024


def kernel(
    columns,
    cores,
    q_hbm,
    kv_hbm,
    lists_hbm,
    out_ref,
    q_ref,
    lists_ref,
    kv,
    q_all,
    bias,
    numer,
    stats,
    numer_in,
    stats_in,
    shares,
    own_sem,
    q_send,
    q_recv,
    n_send,
    n_recv,
    s_send,
    s_recv,
):
    me = lax.axis_index("kcol")
    core = lax.axis_index("qrow")
    tok_dev, features = q_ref.shape
    head_dim = kv.shape[1] // 2
    heads = features // head_dim
    stored = kv.shape[0] // BLK
    all_blocks = stored * columns
    query_blocks = lists_ref.shape[0]
    rows = tok_dev * heads
    unit_cols = LANES // rows
    units = columns // unit_cols
    tile_cols = BLK // cores // tok_dev
    scale = math.log2(math.e) / math.sqrt(head_dim)

    q_load = pltpu.make_async_copy(q_hbm, q_ref, own_sem.at[0])
    q_load.start()
    barrier = pltpu.get_barrier_semaphore()
    for step in range(1, columns):
        pl.semaphore_signal(
            barrier, inc=1, device_id={"kcol": lax.rem(me + step, columns)}
        )

    def rows_of(column):
        return pl.ds(pl.multiple_of(column * rows, rows), rows)

    kv_copy = pltpu.make_async_copy(kv_hbm, kv, own_sem.at[1])
    kv_copy.start()
    lists_load = pltpu.make_async_copy(lists_hbm, lists_ref, own_sem.at[2])
    lists_load.start()

    q_load.wait()
    own = q_ref[...].astype(jnp.float32)
    own = jnp.concatenate(
        [own[:, h * head_dim : (h + 1) * head_dim] for h in range(heads)], axis=0
    )
    q_all[rows_of(me), :] = own.astype(jnp.bfloat16)

    pl.semaphore_wait(barrier, columns - 1)

    my_unit = me // unit_cols
    my_place = lax.rem(me, unit_cols)

    def unit_at(g):
        return lax.rem(my_unit + g, units)

    def column_at(g, j):
        return unit_at(g) * unit_cols + lax.rem(my_place + j, unit_cols)

    def q_copy(peer):
        return pltpu.make_async_remote_copy(
            src_ref=q_all.at[rows_of(me)],
            dst_ref=q_all.at[rows_of(me)],
            send_sem=q_send.at[peer],
            recv_sem=q_recv.at[me],
            device_id={"kcol": peer},
        )

    def q_landed(source):
        return pltpu.make_async_remote_copy(
            src_ref=q_all.at[rows_of(source)],
            dst_ref=q_all.at[rows_of(source)],
            send_sem=q_send.at[source],
            recv_sem=q_recv.at[source],
            device_id={"kcol": source},
        )

    def n_copy(peer, source):
        return pltpu.make_async_remote_copy(
            src_ref=numer.at[rows_of(peer)],
            dst_ref=numer_in.at[rows_of(source)],
            send_sem=n_send.at[peer],
            recv_sem=n_recv.at[source],
            device_id={"kcol": peer},
        )

    def s_copy(peer, source):
        return pltpu.make_async_remote_copy(
            src_ref=stats.at[peer // unit_cols],
            dst_ref=stats_in.at[source],
            send_sem=s_send.at[peer],
            recv_sem=s_recv.at[source],
            device_id={"kcol": peer},
        )

    peers = [(g, j) for g in range(units) for j in range(unit_cols) if g or j]
    for g, j in peers:
        q_copy(column_at(units - g if g else 0, j)).start()

    lists_load.wait()
    for tile in range(query_blocks):
        listed = lists_ref[tile : tile + 1, :]
        for block in range(stored):
            hit = jnp.where(listed == me * stored + block, 0.0, MASKED)
            hit = jnp.max(hit, axis=1, keepdims=True)
            bias[tile, :, block * BLK : (block + 1) * BLK] = jnp.broadcast_to(hit, (8, BLK))

    row_id = lax.broadcasted_iota(jnp.int32, (LANES, LANES), 0)
    lane_id = lax.broadcasted_iota(jnp.int32, (LANES, LANES), 1)
    diagonal = row_id == lane_id
    row_token = core * tok_dev + lax.rem(row_id, tok_dev)
    row_column = row_id // rows

    kv_copy.wait()

    for g in range(units):
        unit = unit_at(g)
        for j in range(unit_cols):
            if g or j:
                q_landed(column_at(g, j)).wait_recv()
        tile = unit * unit_cols // tile_cols
        unit_rows = pl.ds(pl.multiple_of(unit * LANES, LANES), LANES)
        scores = lax.dot_general(
            q_all[unit_rows, :],
            kv[:, :head_dim],
            (((1,), (1,)), ((), ())),
            preferred_element_type=jnp.float32,
        )
        query_pos = (
            (all_blocks - query_blocks) * BLK
            + (unit * unit_cols + row_column) * (cores * tok_dev)
            + row_token
        )
        parts = []
        for block in range(stored):
            part = scores[:, block * BLK : (block + 1) * BLK]
            part = part + bias[tile, 0:1, block * BLK : (block + 1) * BLK]
            if block >= stored - query_blocks:
                key_pos = (me * stored + block) * BLK + lane_id
                part = jnp.where(key_pos <= query_pos, part, MASKED)
            parts.append(part)
        row_max = functools.reduce(jnp.maximum, parts)
        row_max = jnp.max(row_max, axis=1, keepdims=True)
        weights = [jnp.exp2((part - row_max) * scale) for part in parts]
        row_total = jnp.sum(functools.reduce(jnp.add, weights), axis=1, keepdims=True)
        stats[unit, 0:1, :] = jnp.sum(jnp.where(diagonal, row_max, 0.0), axis=0, keepdims=True)
        stats[unit, 1:2, :] = jnp.sum(jnp.where(diagonal, row_total, 0.0), axis=0, keepdims=True)
        for j in range(unit_cols):
            if g or j:
                s_copy(column_at(g, j), me).start()
        summed = lax.dot_general(
            jnp.concatenate([w.astype(jnp.bfloat16) for w in weights], axis=1),
            kv[:, head_dim:],
            (((1,), (0,)), ((), ())),
            preferred_element_type=jnp.float32,
        )
        numer[unit_rows, :] = summed.astype(jnp.bfloat16)
        for j in range(unit_cols):
            if g or j:
                n_copy(column_at(g, j), me).start()

    numer_in[rows_of(me), :] = numer[rows_of(me), :]
    stats_in[me] = stats[my_unit]

    for g, j in peers:
        source = column_at(units - g if g else 0, j)
        s_copy(source, source).wait_recv()
    every_max = stats_in[:, 0, :]
    every_total = stats_in[:, 1, :]
    top = jnp.max(every_max, axis=0, keepdims=True)
    factor = jnp.exp2((every_max - top) * scale)
    factor = factor / jnp.sum(factor * every_total, axis=0, keepdims=True)
    pad = -columns % LANES
    if pad:
        factor = jnp.concatenate([factor, jnp.zeros((pad, LANES), jnp.float32)], axis=0)
    factor = jnp.transpose(factor)
    turned = jnp.zeros((rows, LANES), jnp.float32)
    for place in range(unit_cols):
        turned = jnp.where(my_place == place, factor[place * rows : (place + 1) * rows, :], turned)

    for source in range(columns):
        shares[source * rows : (source + 1) * rows, :] = jnp.broadcast_to(
            turned[:, source : source + 1], (rows, head_dim)
        )

    def share(source):
        part = numer_in[rows_of(source), :].astype(jnp.float32)
        return part * shares[rows_of(source), :]

    total = share(me)
    for g, j in peers:
        source = column_at(units - g if g else 0, j)
        n_copy(source, source).wait_recv()
        total = total + share(source)
    out_ref[...] = jnp.concatenate(
        [total[h * tok_dev : (h + 1) * tok_dev, :] for h in range(heads)], axis=1
    ).astype(out_ref.dtype)

    for g, j in peers:
        peer = column_at(g, j)
        q_copy(peer).wait_send()
        n_copy(peer, me).wait_send()
        s_copy(peer, me).wait_send()


def per_device(columns, cores, queries, key_value, block_lists):
    tok_dev, features = queries.shape
    head_dim = key_value.shape[1] // 2
    all_rows = columns * tok_dev * (features // head_dim)
    query_blocks = block_lists.shape[0]
    units = all_rows // LANES
    dma = pltpu.SemaphoreType.DMA
    hbm = pl.BlockSpec(memory_space=pltpu.HBM)
    return pl.pallas_call(
        functools.partial(kernel, columns, cores),
        out_shape=jax.ShapeDtypeStruct((tok_dev, features), jnp.bfloat16),
        in_specs=[hbm, hbm, hbm],
        out_specs=pl.BlockSpec(memory_space=pltpu.VMEM),
        scratch_shapes=[
            pltpu.VMEM(queries.shape, jnp.bfloat16),
            pltpu.VMEM(block_lists.shape, jnp.int32),
            pltpu.VMEM(key_value.shape, jnp.bfloat16),
            pltpu.VMEM((all_rows, head_dim), jnp.bfloat16),
            pltpu.VMEM((query_blocks, 8, key_value.shape[0]), jnp.float32),
            pltpu.VMEM((all_rows, head_dim), jnp.bfloat16),
            pltpu.VMEM((units, 2, LANES), jnp.float32),
            pltpu.VMEM((all_rows, head_dim), jnp.bfloat16),
            pltpu.VMEM((columns, 2, LANES), jnp.float32),
            pltpu.VMEM((all_rows, head_dim), jnp.float32),
            dma((3,)),
            dma((columns,)),
            dma((columns,)),
            dma((columns,)),
            dma((columns,)),
            dma((columns,)),
            dma((columns,)),
        ],
        compiler_params=pltpu.CompilerParams(
            collective_id=0, has_side_effects=True, vmem_limit_bytes=VMEM_LIMIT
        ),
    )(queries, key_value, block_lists)


def solution(mesh):
    placed = (P(("groups", "kcol", "qrow"), None), P(("groups", "kcol"), None), P("groups", None))
    return jax.shard_map(
        functools.partial(per_device, mesh.shape["kcol"], mesh.shape["qrow"]),
        mesh=mesh,
        in_specs=placed,
        out_specs=P(("groups", "kcol", "qrow"), None),
        check_vma=False,
    )
```

```python
import functools
import math

import jax
import jax.numpy as jnp
from jax import lax
from jax.experimental import pallas as pl
from jax.experimental.pallas import tpu as pltpu
from jax.sharding import PartitionSpec as P

BLK = 128
LANES = 128
MASKED = -(2.0**100)
VMEM_LIMIT = 127 * 512 * 1024


def kernel(
    columns,
    cores,
    q_hbm,
    kv_hbm,
    lists_hbm,
    out_ref,
    q_ref,
    lists_ref,
    kv,
    q_all,
    bias,
    numer,
    stats,
    numer_in,
    stats_in,
    shares,
    own_sem,
    q_send,
    q_recv,
    n_send,
    n_recv,
    s_send,
    s_recv,
):
    me = lax.axis_index("kcol")
    core = lax.axis_index("qrow")
    tok_dev, features = q_ref.shape
    head_dim = kv.shape[1] // 2
    heads = features // head_dim
    stored = kv.shape[0] // BLK
    all_blocks = stored * columns
    query_blocks = lists_ref.shape[0]
    rows = tok_dev * heads
    unit_cols = LANES // rows
    units = columns // unit_cols
    tile_cols = BLK // cores // tok_dev
    scale = math.log2(math.e) / math.sqrt(head_dim)

    q_load = pltpu.make_async_copy(q_hbm, q_ref, own_sem.at[0])
    q_load.start()
    barrier = pltpu.get_barrier_semaphore()
    for step in range(1, columns):
        pl.semaphore_signal(
            barrier, inc=1, device_id={"kcol": lax.rem(me + step, columns)}
        )

    def rows_of(column):
        return pl.ds(pl.multiple_of(column * rows, rows), rows)

    kv_copy = pltpu.make_async_copy(kv_hbm, kv, own_sem.at[1])
    kv_copy.start()
    lists_load = pltpu.make_async_copy(lists_hbm, lists_ref, own_sem.at[2])
    lists_load.start()

    q_load.wait()
    own = q_ref[...].astype(jnp.float32)
    own = jnp.concatenate(
        [own[:, h * head_dim : (h + 1) * head_dim] for h in range(heads)], axis=0
    )
    q_all[rows_of(me), :] = own.astype(jnp.bfloat16)

    pl.semaphore_wait(barrier, columns - 1)

    my_unit = me // unit_cols
    my_place = lax.rem(me, unit_cols)

    def unit_at(g):
        return lax.rem(my_unit + g, units)

    def column_at(g, j):
        return unit_at(g) * unit_cols + lax.rem(my_place + j, unit_cols)

    def q_copy(peer):
        return pltpu.make_async_remote_copy(
            src_ref=q_all.at[rows_of(me)],
            dst_ref=q_all.at[rows_of(me)],
            send_sem=q_send.at[peer],
            recv_sem=q_recv.at[me],
            device_id={"kcol": peer},
        )

    def q_landed(source):
        return pltpu.make_async_remote_copy(
            src_ref=q_all.at[rows_of(source)],
            dst_ref=q_all.at[rows_of(source)],
            send_sem=q_send.at[source],
            recv_sem=q_recv.at[source],
            device_id={"kcol": source},
        )

    def n_copy(peer, source):
        return pltpu.make_async_remote_copy(
            src_ref=numer.at[rows_of(peer)],
            dst_ref=numer_in.at[rows_of(source)],
            send_sem=n_send.at[peer],
            recv_sem=n_recv.at[source],
            device_id={"kcol": peer},
        )

    def s_copy(peer, source):
        return pltpu.make_async_remote_copy(
            src_ref=stats.at[peer // unit_cols],
            dst_ref=stats_in.at[source],
            send_sem=s_send.at[peer],
            recv_sem=s_recv.at[source],
            device_id={"kcol": peer},
        )

    peers = [(g, j) for g in range(units) for j in range(unit_cols) if g or j]
    for g, j in peers:
        q_copy(column_at(units - g if g else 0, j)).start()

    lists_load.wait()
    for tile in range(query_blocks):
        listed = lists_ref[tile : tile + 1, :]
        for block in range(stored):
            hit = jnp.where(listed == me * stored + block, 0.0, MASKED)
            hit = jnp.max(hit, axis=1, keepdims=True)
            bias[tile, :, block * BLK : (block + 1) * BLK] = jnp.broadcast_to(hit, (8, BLK))

    row_id = lax.broadcasted_iota(jnp.int32, (LANES, LANES), 0)
    lane_id = lax.broadcasted_iota(jnp.int32, (LANES, LANES), 1)
    diagonal = row_id == lane_id
    row_token = core * tok_dev + lax.rem(row_id, tok_dev)
    row_column = row_id // rows

    kv_copy.wait()

    for g in range(units):
        unit = unit_at(g)
        for j in range(unit_cols):
            if g or j:
                q_landed(column_at(g, j)).wait_recv()
        tile = unit * unit_cols // tile_cols
        unit_rows = pl.ds(pl.multiple_of(unit * LANES, LANES), LANES)
        scores = lax.dot_general(
            q_all[unit_rows, :],
            kv[:, :head_dim],
            (((1,), (1,)), ((), ())),
            preferred_element_type=jnp.float32,
        )
        query_pos = (
            (all_blocks - query_blocks) * BLK
            + (unit * unit_cols + row_column) * (cores * tok_dev)
            + row_token
        )
        parts = []
        for block in range(stored):
            part = scores[:, block * BLK : (block + 1) * BLK]
            part = part + bias[tile, 0:1, block * BLK : (block + 1) * BLK]
            if block >= stored - query_blocks:
                key_pos = (me * stored + block) * BLK + lane_id
                part = jnp.where(key_pos <= query_pos, part, MASKED)
            parts.append(part)
        row_max = functools.reduce(jnp.maximum, parts)
        row_max = jnp.max(row_max, axis=1, keepdims=True)
        weights = [jnp.exp2((part - row_max) * scale) for part in parts]
        row_total = jnp.sum(functools.reduce(jnp.add, weights), axis=1, keepdims=True)
        stats[unit, 0:1, :] = jnp.sum(jnp.where(diagonal, row_max, 0.0), axis=0, keepdims=True)
        stats[unit, 1:2, :] = jnp.sum(jnp.where(diagonal, row_total, 0.0), axis=0, keepdims=True)
        for j in range(unit_cols):
            if g or j:
                s_copy(column_at(g, j), me).start()
        summed = lax.dot_general(
            jnp.concatenate([w.astype(jnp.bfloat16) for w in weights], axis=1),
            kv[:, head_dim:],
            (((1,), (0,)), ((), ())),
            preferred_element_type=jnp.float32,
        )
        numer[unit_rows, :] = summed.astype(jnp.bfloat16)
        for j in range(unit_cols):
            if g or j:
                n_copy(column_at(g, j), me).start()

    numer_in[rows_of(me), :] = numer[rows_of(me), :]
    stats_in[me] = stats[my_unit]

    for g, j in peers:
        source = column_at(units - g if g else 0, j)
        s_copy(source, source).wait_recv()
    every_max = stats_in[:, 0, :]
    every_total = stats_in[:, 1, :]
    top = jnp.max(every_max, axis=0, keepdims=True)
    factor = jnp.exp2((every_max - top) * scale)
    factor = factor / jnp.sum(factor * every_total, axis=0, keepdims=True)
    mine = row_id[:rows] + my_place * rows == lane_id[:rows]
    for source in range(columns):
        picked = jnp.where(mine, factor[source : source + 1, :], 0.0)
        shares[source * rows : (source + 1) * rows, :] = jnp.broadcast_to(
            jnp.sum(picked, axis=1, keepdims=True), (rows, head_dim)
        )

    def share(source):
        part = numer_in[rows_of(source), :].astype(jnp.float32)
        return part * shares[rows_of(source), :]

    total = share(me)
    for g, j in peers:
        source = column_at(units - g if g else 0, j)
        n_copy(source, source).wait_recv()
        total = total + share(source)
    out_ref[...] = jnp.concatenate(
        [total[h * tok_dev : (h + 1) * tok_dev, :] for h in range(heads)], axis=1
    ).astype(out_ref.dtype)

    for g, j in peers:
        peer = column_at(g, j)
        q_copy(peer).wait_send()
        n_copy(peer, me).wait_send()
        s_copy(peer, me).wait_send()


def per_device(columns, cores, queries, key_value, block_lists):
    tok_dev, features = queries.shape
    head_dim = key_value.shape[1] // 2
    all_rows = columns * tok_dev * (features // head_dim)
    query_blocks = block_lists.shape[0]
    units = all_rows // LANES
    dma = pltpu.SemaphoreType.DMA
    hbm = pl.BlockSpec(memory_space=pltpu.HBM)
    return pl.pallas_call(
        functools.partial(kernel, columns, cores),
        out_shape=jax.ShapeDtypeStruct((tok_dev, features), jnp.bfloat16),
        in_specs=[hbm, hbm, hbm],
        out_specs=pl.BlockSpec(memory_space=pltpu.VMEM),
        scratch_shapes=[
            pltpu.VMEM(queries.shape, jnp.bfloat16),
            pltpu.VMEM(block_lists.shape, jnp.int32),
            pltpu.VMEM(key_value.shape, jnp.bfloat16),
            pltpu.VMEM((all_rows, head_dim), jnp.bfloat16),
            pltpu.VMEM((query_blocks, 8, key_value.shape[0]), jnp.float32),
            pltpu.VMEM((all_rows, head_dim), jnp.bfloat16),
            pltpu.VMEM((units, 2, LANES), jnp.float32),
            pltpu.VMEM((all_rows, head_dim), jnp.bfloat16),
            pltpu.VMEM((columns, 2, LANES), jnp.float32),
            pltpu.VMEM((all_rows, head_dim), jnp.float32),
            dma((3,)),
            dma((columns,)),
            dma((columns,)),
            dma((columns,)),
            dma((columns,)),
            dma((columns,)),
            dma((columns,)),
        ],
        compiler_params=pltpu.CompilerParams(
            collective_id=0, has_side_effects=True, vmem_limit_bytes=VMEM_LIMIT
        ),
    )(queries, key_value, block_lists)


def solution(mesh):
    placed = (P(("groups", "kcol", "qrow"), None), P(("groups", "kcol"), None), P("groups", None))
    return jax.shard_map(
        functools.partial(per_device, mesh.shape["kcol"], mesh.shape["qrow"]),
        mesh=mesh,
        in_specs=placed,
        out_specs=P(("groups", "kcol", "qrow"), None),
        check_vma=False,
    )
```
